256 devices in a mesh: row: 16 (over y, z_lo, core), col: 16 (over z_hi, x).
Axes of the slice: x: 4, y: 4, z: 8 (z_hi: 4, z_lo: 2; z = z_hi * 2 + z_lo), core: 2. Of those that a mesh axis runs over, the one named last changes fastest.
Arguments:
- node_feats: bfloat16 [65536, 256], P(('col', 'row')), may hold values from -6 to 6
- weight: bfloat16 [256, 256], replicated, may hold values from -0.375 to 0.375
- bias: float32 [256], replicated, may hold values from -3 to 3
- cotangent: bfloat16 [65536, 256], P(('row', 'col')), may hold values from -6 to 6
- tiles: bfloat16 [16, 16, 192, 128, 128], P('row', 'col'), as said below
- coords: int32 [16, 16, 192, 2], P('row', 'col'), may hold values from 0 to 31, as said below
- counts: int32 [16, 16], P('row', 'col'), may hold values from 24 to 192, as said below
Outputs:
- activations: bfloat16 [65536, 256], P(('row', 'col'))
- weight_grad: float32 [256, 256], replicated
- bias_grad: float32 [256], replicated
- feats_grad: bfloat16 [65536, 256], P(('col', 'row'))
The draws below stay inside these ranges and needn't reach their ends.
Inputs may be any that keep to these rules, and one draw needn't show every extreme that they name: `coords`: within one block the 192 slots name distinct tile positions; the row is below 32 and the column below 32, also in slots that are not live; every block holds the position (31, 31) in some slot. Live slot counts of the blocks vary widely; some block has all 192 slots live. `tiles`: entries are zero or positive.
All inputs are finite; a program needn't handle non-finite values.
Results may differ from the reference program's by a relative error of at most 0.008.
Values may be sent and summed in bfloat16 or wider, within the bound.
A program may use at most 128 MiB of HBM per device.

```python
import jax
import jax.numpy as jnp
from jax import lax

F = 256
TILE = 128
R = 256
NODES = 65536
TBR = 32
TBC = 32
CAP = 192
N_ROW = 16
N_COL = 16


def draw_tiles(key, part):
    key = jax.random.fold_in(key, 37)
    key_keep, key_mag = jax.random.split(key)
    shape = (N_ROW, N_COL, CAP, TILE, TILE)
    keep = jax.random.uniform(key_keep, shape, dtype=jnp.float32) < 0.25
    mags = jax.random.uniform(key_mag, shape, dtype=jnp.float32, minval=0.5, maxval=1.5)
    factor = (4.0 * R / (CAP * TILE * TILE)) ** 0.5
    return jnp.where(keep, mags * factor, 0.0).astype(jnp.bfloat16)


def draw_coords(key, part):
    key = jax.random.fold_in(key, 11)
    keys = jax.random.split(key, N_ROW * N_COL)

    def one_block(block_key):
        key_perm, key_shift = jax.random.split(block_key)
        corner = jnp.array([TBR * TBC - 1], dtype=jnp.int32)
        others = jax.random.permutation(key_perm, TBR * TBC - 1)[:CAP - 1].astype(jnp.int32)
        order = jnp.concatenate([corner, others])
        shift = jax.random.randint(key_shift, (), 0, CAP)
        order = jnp.roll(order, shift)
        return jnp.stack([order // TBC, order % TBC], axis=1)
    return jax.vmap(one_block)(keys).reshape(N_ROW, N_COL, CAP, 2)


def draw_counts(key, part):
    key = jax.random.fold_in(key, 23)
    key_div, key_first, key_second = jax.random.split(key, 3)
    total = N_ROW * N_COL
    divisors = jax.random.randint(key_div, (total,), 1, 9)
    values = (CAP // divisors).astype(jnp.int32)
    first = jax.random.randint(key_first, (), 0, total)
    second = (first + 1 + jax.random.randint(key_second, (), 0, total - 1)) % total
    values = values.at[first].set(CAP).at[second].set(CAP // 8)
    return values.reshape(N_ROW, N_COL)


def level_of(own_key, shape, shards, low, largest):
    gain, own = 1.0, jax.random.fold_in(own_key, 6)
    for axis_at, parts in shards:
        steps = jnp.exp(jax.random.uniform(jax.random.fold_in(own, axis_at), (parts,), jnp.float32, low / len(shards), largest / len(shards)))
        gain = gain * jnp.repeat(steps, shape[axis_at] // parts).reshape([-1 if axis == axis_at else 1 for axis in range(len(shape))])
    return gain


def gaussian(own_key, extent, width, bound, shards=(), kind=jnp.bfloat16):
    level = level_of(own_key, extent, shards, -0.22, 0.18) if shards else 1.0
    entries = jax.random.normal(own_key, extent, jnp.float32) * width * level
    return jnp.minimum(jnp.maximum(entries, -bound), bound).astype(kind)


def setup_inputs(seed: int = 0) -> dict:
    seeds = jax.random.split(jax.random.key(seed), 8)
    node_feats = gaussian(seeds[0], (NODES, F), 1.0, 6.0, ((0, 256),))
    weight = gaussian(seeds[1], (F, F), F ** -0.5, 0.375)
    bias = gaussian(seeds[2], (F,), 0.5, 3.0, (), jnp.float32)
    cotangent = gaussian(seeds[3], (NODES, F), 1.0, 6.0, ((0, 256),))
    tiles = draw_tiles(jax.random.fold_in(seeds[7], 71), 0)
    coords = draw_coords(jax.random.fold_in(seeds[7], 71), 0)
    counts = draw_counts(jax.random.fold_in(seeds[7], 71), 0)
    return {"node_feats": node_feats, "weight": weight, "bias": bias, "cotangent": cotangent, "tiles": tiles, "coords": coords, "counts": counts}


def reference(node_feats, weight, bias, cotangent, tiles, coords, counts):
    feat_tiles = node_feats.reshape(NODES // TILE, TILE, F)
    slot_ids = jnp.arange(CAP, dtype=jnp.int32)

    def forward_block(index, acc):
        brow = index // N_COL
        bcol = index % N_COL
        values = tiles[brow, bcol].astype(jnp.float32)
        places = coords[brow, bcol]
        live = slot_ids < counts[brow, bcol]
        taken = feat_tiles[bcol * TBC + places[:, 1]].astype(jnp.float32)
        product = jnp.einsum("bij,bjf->bif", values, taken)
        product = jnp.where(live[:, None, None], product, 0.0)
        return acc.at[brow * TBR + places[:, 0]].add(product)

    sums = lax.fori_loop(0, N_ROW * N_COL, forward_block, jnp.zeros((NODES // TILE, TILE, F), jnp.float32))
    aggregated = sums.reshape(NODES, F).astype(jnp.bfloat16)
    pre = jnp.dot(aggregated, weight, preferred_element_type=jnp.float32) + bias
    gate = jax.nn.sigmoid(pre)
    activations = (pre * gate).astype(jnp.bfloat16)
    pre_grad = (cotangent.astype(jnp.float32) * gate * (1.0 + pre * (1.0 - gate))).astype(jnp.bfloat16)
    weight_grad = jnp.dot(aggregated.T, pre_grad, preferred_element_type=jnp.float32)
    bias_grad = jnp.sum(pre_grad.astype(jnp.float32), axis=0)
    agg_grad = jnp.dot(pre_grad, weight.T, preferred_element_type=jnp.float32).astype(jnp.bfloat16)
    grad_tiles = agg_grad.reshape(NODES // TILE, TILE, F)

    def backward_block(index, acc):
        brow = index // N_COL
        bcol = index % N_COL
        values = tiles[brow, bcol].astype(jnp.float32)
        places = coords[brow, bcol]
        live = slot_ids < counts[brow, bcol]
        taken = grad_tiles[brow * TBR + places[:, 0]].astype(jnp.float32)
        product = jnp.einsum("bji,bjf->bif", values, taken)
        product = jnp.where(live[:, None, None], product, 0.0)
        return acc.at[bcol * TBC + places[:, 1]].add(product)

    back = lax.fori_loop(0, N_ROW * N_COL, backward_block, jnp.zeros((NODES // TILE, TILE, F), jnp.float32))
    feats_grad = back.reshape(NODES, F).astype(jnp.bfloat16)
    return activations, weight_grad, bias_grad, feats_grad
```

```python
import functools

import jax
import jax.numpy as jnp
from jax import lax
from jax.experimental import pallas as pl
from jax.experimental.pallas import tpu as pltpu
from jax.sharding import PartitionSpec as P

F = 256
H = 128
T = 128
SLOTS = 192
TR = 32
BF = jnp.bfloat16
F32 = jnp.float32
MESH = pl.DeviceIdType.MESH
UNROLL = 16
WR = 24


def slot_order(coords_ref, count, meta):
    slot = lax.broadcasted_iota(jnp.int32, (SLOTS, 1), 0)
    lane = lax.broadcasted_iota(jnp.int32, (SLOTS, 256), 1)
    sub = lax.broadcasted_iota(jnp.int32, (SLOTS, 256), 0)
    rows = coords_ref[:, 0:1]
    cols = coords_ref[:, 1:2]
    live = slot < count
    value = slot + rows * 256 + cols * 8192
    for at, (major, minor) in enumerate(((rows, cols), (cols, rows))):
        key = jnp.where(live, major * TR + minor, TR * TR + slot)
        across = jnp.sum(jnp.where(sub == lane, key, 0), axis=0, keepdims=True)
        less = jnp.logical_and(across < key, lane < SLOTS)
        rank = jnp.sum(jnp.where(less, 1, 0), axis=1, keepdims=True)
        meta[at : at + 1, :] = jnp.sum(jnp.where(rank == lane, value, 0), axis=0, keepdims=True)
        upto = jnp.logical_and(major <= lane, live)
        meta[at + 2 : at + 3, :] = jnp.sum(jnp.where(upto, 1, 0), axis=0, keepdims=True) - 1


def tile_sums(order, tiles, source, prefix, out, back):
    def place(slot):
        word = order[1 if back else 0, slot]
        index = lax.rem(word, 256)
        row = lax.rem(lax.div(word, 256), TR)
        col = lax.div(word, 8192)
        return (index, col, row) if back else (index, row, col)

    def product(index, read):
        dims = (((0,), (0,)), ((), ())) if back else (((1,), (0,)), ((), ()))
        return lax.dot_general(tiles[index], source[read], dims, preferred_element_type=F32)

    def step(block, acc):
        start = block * UNROLL
        places = [place(start + u) for u in range(UNROLL)]
        before = place(jnp.maximum(start - 1, 0))[1]
        products = [product(index, read) for index, _, read in places]
        for u in range(UNROLL):
            write = places[u][1]
            acc = jnp.where(write == before, acc, 0.0) + products[u]
            prefix[start + u] = acc.astype(BF)
            before = write
        return acc

    lax.fori_loop(0, SLOTS // UNROLL, step, jnp.zeros((T, H), F32))

    def take(r, _):
        last = order[3 if back else 2, r]
        previous = jnp.where(r == 0, -1, order[3 if back else 2, jnp.maximum(r - 1, 0)])
        value = prefix[jnp.maximum(last, 0)]
        out[r] = jnp.where(last > previous, value, jnp.zeros_like(value))
        return 0

    lax.fori_loop(0, TR, take, 0, unroll=4)


def kernel(
    feats_in, weight, bias, cotangent, tiles_hbm, coords, counts,
    activations, weight_grad, bias_grad, feats_grad,
    tiles, meta, order, prefix, f0, f1, s0, s1, x0, x1, zs0, zs1, zr0, zr1, own0, own1, agg, g0, g1,
    cr0, cr1, rs0, rs1, rr0, rr1, ws, wx, wzs, wz, wcs, wcr, wrs, wr, wout,
    local_sem, f_send, f_recv, fc_send, fc_recv, x_send, x_recv, z_send, z_recv,
    gz_send, gz_recv, gx_send, gx_recv, c_send, c_recv, r_send, r_recv,
    wx_send, wx_recv, wz_send, wz_recv, wc_send, wc_recv, wr_send, wr_recv,
    va_send, va_recv, vb_send, vb_recv,
):
    row, col = lax.axis_index("row"), lax.axis_index("col")
    y, zl, core = lax.div(row, 4), lax.rem(lax.div(row, 2), 2), lax.rem(row, 2)
    zh, x = lax.div(col, 4), lax.rem(col, 4)

    def row_at(dy, dz, dc):
        return (lax.rem(y + dy, 4) * 2 + lax.rem(zl + dz, 2)) * 2 + lax.rem(core + dc, 2)

    def col_at(dz, dx):
        return lax.rem(zh + dz, 4) * 4 + lax.rem(x + dx, 4)

    sibling = (row_at(0, 0, 1), col)
    chips = [(dy, dz) for dy in range(4) for dz in range(2) if (dy, dz) != (0, 0)]
    sends = []

    def send(src, dst, ssem, rsem, device):
        copy = pltpu.make_async_remote_copy(
            src_ref=src, dst_ref=dst, send_sem=ssem, recv_sem=rsem, device_id=device, device_id_type=MESH
        )
        copy.start()
        sends.append(copy)
        return copy

    load = pltpu.make_async_copy(tiles_hbm, tiles, local_sem.at[0])
    load.start()

    partners = [sibling]
    partners += [(row_at(dy, dz, 0), col) for dy, dz in chips]
    partners += [(row, col_at(0, d)) for d in range(1, 4)]
    partners += [(row, col_at(d, 0)) for d in range(1, 4)]
    barrier = pltpu.get_barrier_semaphore()
    for device in partners:
        pl.semaphore_signal(barrier, inc=1, device_id=device, device_id_type=MESH)
    feats = (f0, f1)
    for h in range(2):
        feats[h][pl.ds(2 * row, 2)] = feats_in[:, h * H : (h + 1) * H].reshape(2, T, H)
    pl.semaphore_wait(barrier, len(partners))

    got = {}
    for h in range(2):
        mine = feats[h].at[pl.ds(2 * row, 2)]
        for n, (dy, dz) in enumerate(chips):
            got[h, n] = send(mine, mine, f_send.at[h, n], f_recv.at[h, n], (row_at(dy, dz, 0), col))
        got[h, 7] = send(mine, mine, fc_send.at[h, 7], fc_recv.at[h, 7], sibling)

    slot_order(coords, counts[0, 0], meta)
    move = pltpu.make_async_copy(meta, order, local_sem.at[1])
    move.start()
    move.wait()
    load.wait()

    sums = (s0, s1)
    xr = (x0, x1)
    zsend = (zs0, zs1)
    zrecv = (zr0, zr1)
    own = (own0, own1)

    def gather_features(h):
        passed = []
        for n, (dy, dz) in enumerate(chips):
            got[h, n].wait_recv()
            came = feats[h].at[pl.ds(2 * row_at(4 - dy, dz, 0), 2)]
            passed.append(send(came, came, fc_send.at[h, n], fc_recv.at[h, n], sibling))
        got[h, 7].wait_recv()
        for copy in passed:
            copy.wait_recv()

    xcopies = {}

    def scatter_x(h):
        for k in (2, 1, 3, 0):
            for d in (2, 1, 3):
                at = pl.ds(2 * col_at(k, d), 2)
                xcopies[h, k, d] = send(
                    sums[h].at[at], xr[h].at[d - 1, k], x_send.at[h, d - 1, k], x_recv.at[h, d - 1, k],
                    (row, col_at(0, d)),
                )

    zcopies = {}

    def scatter_z(h):
        for k in (2, 1, 3, 0):
            total = sums[h][pl.ds(2 * col_at(k, 0), 2)].astype(F32)
            for d in range(1, 4):
                xcopies[h, k, d].wait_recv()
                total += xr[h][d - 1, k].astype(F32)
            if k:
                zsend[h][k - 1] = total.astype(BF)
                zcopies[h, k] = send(
                    zsend[h].at[k - 1], zrecv[h].at[k - 1], z_send.at[h, k - 1], z_recv.at[h, k - 1],
                    (row, col_at(k, 0)),
                )
            else:
                own[h][...] = total

    def finish_aggregate(h):
        total = own[h][...]
        for k in range(1, 4):
            zcopies[h, k].wait_recv()
            total += zrecv[h][k - 1].astype(F32)
        agg[:, h * H : (h + 1) * H] = total.reshape(2 * T, H).astype(BF)

    gather_features(0)
    tile_sums(order, tiles, f0, prefix, s0, False)
    scatter_x(0)
    gather_features(1)
    tile_sums(order, tiles, f1, prefix, s1, False)
    scatter_x(1)
    scatter_z(0)
    scatter_z(1)
    finish_aggregate(0)
    finish_aggregate(1)

    pre = jnp.dot(agg[...], weight[...], preferred_element_type=F32) + bias[...]
    gate = jax.nn.sigmoid(pre)
    pre_grad = (cotangent[...].astype(F32) * gate * (1.0 + pre * (1.0 - gate))).astype(BF)
    agg_grad = lax.dot_general(
        pre_grad, weight[...], (((1,), (1,)), ((), ())), preferred_element_type=F32
    ).astype(BF)
    grads = (g0, g1)
    for h in range(2):
        grads[h][pl.ds(2 * col, 2)] = agg_grad[:, h * H : (h + 1) * H].reshape(2, T, H)

    gz = {}
    gx = {}

    def spread_x(h, k):
        came = grads[h].at[pl.ds(2 * col_at(4 - k if k else 0, 0), 2)]
        for d in (2, 1, 3):
            gx[h, k, d] = send(
                came, came, gx_send.at[h, k, d - 1], gx_recv.at[h, k, d - 1], (row, col_at(0, d))
            )

    for h in range(2):
        mine = grads[h].at[pl.ds(2 * col, 2)]
        for k in (2, 1, 3):
            gz[h, k] = send(mine, mine, gz_send.at[h, k - 1], gz_recv.at[h, k - 1], (row, col_at(k, 0)))
        spread_x(h, 0)

    activations[...] = (pre * gate).astype(BF)
    part = lax.dot_general(agg[...], pre_grad, (((0,), (0,)), ((), ())), preferred_element_type=F32)
    bias_part = jnp.broadcast_to(jnp.sum(pre_grad.astype(F32), axis=0, keepdims=True), (8, F))
    for a in range(4):
        for b in range(4):
            ws[a, b, 0:16, :] = part[64 * a + 16 * b : 64 * a + 16 * b + 16, :]
            ws[a, b, 16:WR, :] = bias_part

    for k in (1, 3, 2):
        gz[0, k].wait_recv()
        spread_x(0, k)
    for k in (1, 3, 2):
        gz[1, k].wait_recv()
        spread_x(1, k)

    wxc = [
        send(ws.at[lax.rem(x + d, 4)], wx.at[x], wx_send.at[d - 1], wx_recv.at[d - 1], (row, col_at(0, d)))
        for d in range(1, 4)
    ]
    wx[x] = ws[x]

    def gathered(h):
        for k in range(4):
            for d in range(1, 4):
                gx[h, k, d].wait_recv()

    cr = (cr0, cr1)
    rsend = (rs0, rs1)
    rrecv = (rr0, rr1)
    ccopies = {}
    rcopies = {}
    order_out = [(2, 1), (2, 0), (1, 1), (3, 1), (1, 0), (3, 0), (0, 1), (0, 0)]

    def scatter_core(h):
        for n, (dy, dz) in enumerate(order_out):
            at = pl.ds(2 * row_at(dy, dz, 1), 2)
            ccopies[h, n] = send(sums[h].at[at], cr[h].at[n], c_send.at[h, n], c_recv.at[h, n], sibling)

    def scatter_row(h):
        for n, (dy, dz) in enumerate(order_out):
            ccopies[h, n].wait_recv()
            total = sums[h][pl.ds(2 * row_at(dy, dz, 0), 2)].astype(F32) + cr[h][n].astype(F32)
            if n < 7:
                rsend[h][n] = total.astype(BF)
                rcopies[h, n] = send(
                    rsend[h].at[n], rrecv[h].at[n], r_send.at[h, n], r_recv.at[h, n], (row_at(dy, dz, 0), col)
                )
            else:
                own[h][...] = total

    def finish_feats(h):
        total = own[h][...]
        for n in range(7):
            rcopies[h, n].wait_recv()
            total += rrecv[h][n].astype(F32)
        feats_grad[:, h * H : (h + 1) * H] = total.reshape(2 * T, H).astype(BF)

    for copy in xcopies.values():
        copy.wait_send()
    early = {id(copy) for copy in xcopies.values()}

    gathered(0)
    tile_sums(order, tiles, g0, prefix, s0, True)
    scatter_core(0)

    for copy in wxc:
        copy.wait_recv()
    wzs[...] = ((wx[0] + wx[1]) + wx[2]) + wx[3]
    wzc = [
        send(wzs.at[lax.rem(zh + k, 4)], wz.at[zh], wz_send.at[k - 1], wz_recv.at[k - 1], (row, col_at(k, 0)))
        for k in range(1, 4)
    ]
    wz[zh] = wzs[zh]
    scatter_row(0)

    gathered(1)
    tile_sums(order, tiles, g1, prefix, s1, True)
    scatter_core(1)

    for copy in wzc:
        copy.wait_recv()
    wcs[...] = ((wz[0] + wz[1]) + wz[2]) + wz[3]
    wcc = send(wcs, wcr, wc_send.at[0], wc_recv.at[0], sibling)
    scatter_row(1)
    wcc.wait_recv()
    chip = y * 2 + zl
    wrs[...] = wcs[...] + wcr[...]
    wrc = [
        send(wrs, wr.at[chip], wr_send.at[n], wr_recv.at[n], (row_at(dy, dz, 0), col))
        for n, (dy, dz) in enumerate(chips)
    ]
    wr[chip] = wrs[...]
    finish_feats(0)
    for copy in wrc:
        copy.wait_recv()
    total = wr[0]
    for n in range(1, 8):
        total += wr[n]
    bias_grad[...] = total[16:17, :]
    wout[x, zh] = total[0:16, :]
    vac = [
        send(wout.at[x, zh], wout.at[x, zh], va_send.at[k - 1], va_recv.at[k - 1], (row, col_at(k, 0)))
        for k in range(1, 4)
    ]
    finish_feats(1)
    for copy in vac:
        copy.wait_recv()
    vbc = [
        send(wout.at[x], wout.at[x], vb_send.at[d - 1], vb_recv.at[d - 1], (row, col_at(0, d)))
        for d in range(1, 4)
    ]
    for copy in vbc:
        copy.wait_recv()
    weight_grad[...] = wout[...].reshape(F, F)
    for copy in sends:
        if id(copy) not in early:
            copy.wait_send()


def body(node_feats, weight, bias, cotangent, tiles, coords, counts):
    vmem = pl.BlockSpec(memory_space=pltpu.VMEM)
    half = (TR, T, H)
    dma = pltpu.SemaphoreType.DMA
    pair = lambda shape, dtype=BF: [pltpu.VMEM(shape, dtype)] * 2
    both = lambda shape: [dma(shape), dma(shape)]
    activations, weight_grad, bias_grad, feats_grad = pl.pallas_call(
        kernel,
        out_shape=(
            jax.ShapeDtypeStruct((2 * T, F), BF),
            jax.ShapeDtypeStruct((F, F), F32),
            jax.ShapeDtypeStruct((1, F), F32),
            jax.ShapeDtypeStruct((2 * T, F), BF),
        ),
        in_specs=[vmem, vmem, vmem, vmem, pl.BlockSpec(memory_space=pl.ANY), vmem,
                  pl.BlockSpec(memory_space=pltpu.SMEM)],
        out_specs=(vmem, vmem, vmem, vmem),
        scratch_shapes=[
            pltpu.VMEM((SLOTS, T, T), BF),
            pltpu.VMEM((8, 256), jnp.int32),
            pltpu.SMEM((8, 256), jnp.int32),
            pltpu.VMEM((SLOTS, T, H), BF),
            *pair(half),
            *pair(half),
            *pair((3, 4, 2, T, H)),
            *pair((3, 2, T, H)),
            *pair((3, 2, T, H)),
            *pair((2, T, H), F32),
            pltpu.VMEM((2 * T, F), BF),
            *pair(half),
            *pair((8, 2, T, H)),
            *pair((7, 2, T, H)),
            *pair((7, 2, T, H)),
            pltpu.VMEM((4, 4, WR, F), F32),
            pltpu.VMEM((4, 4, WR, F), F32),
            pltpu.VMEM((4, WR, F), F32),
            pltpu.VMEM((4, WR, F), F32),
            pltpu.VMEM((WR, F), F32),
            pltpu.VMEM((WR, F), F32),
            pltpu.VMEM((WR, F), F32),
            pltpu.VMEM((8, WR, F), F32),
            pltpu.VMEM((4, 4, 16, F), F32),
            dma((2,)),
            *both((2, 7)),
            *both((2, 8)),
            *both((2, 3, 4)),
            *both((2, 3)),
            *both((2, 3)),
            *both((2, 4, 3)),
            *both((2, 8)),
            *both((2, 7)),
            *both((3,)),
            *both((3,)),
            *both((1,)),
            *both((7,)),
            *both((3,)),
            *both((3,)),
        ],
        compiler_params=pltpu.CompilerParams(
            collective_id=0, has_side_effects=True, vmem_limit_bytes=48 * 2**20
        ),
    )(node_feats, weight, bias.reshape(1, F), cotangent, tiles.reshape(SLOTS, T, T),
      coords.reshape(SLOTS, 2), counts)
    return activations, weight_grad, bias_grad.reshape(F), feats_grad


def solution(mesh):
    return jax.shard_map(
        body,
        mesh=mesh,
        in_specs=(
            P(("col", "row"), None),
            P(),
            P(),
            P(("row", "col"), None),
            P("row", "col", None, None, None),
            P("row", "col", None, None),
            P("row", "col"),
        ),
        out_specs=(P(("row", "col"), None), P(), P(), P(("col", "row"), None)),
        check_vma=False,
    )
```

```python
import functools

import jax
import jax.numpy as jnp
from jax import lax
from jax.experimental import pallas as pl
from jax.experimental.pallas import tpu as pltpu
from jax.sharding import PartitionSpec as P

F = 256
H = 128
T = 128
SLOTS = 192
TR = 32
BF = jnp.bfloat16
F32 = jnp.float32
MESH = pl.DeviceIdType.MESH
UNROLL = 16


class Sent:
    def __init__(self, copy):
        self.copy, self.here, self.there = copy, False, False

    def wait_recv(self):
        if not self.here:
            self.copy.wait_recv()
        self.here = True

    def wait(self):
        if not self.here:
            self.copy.wait()
        self.here = True

    def wait_send(self):
        if not self.there:
            self.copy.wait_send()
        self.there = True


def slot_order(coords_ref, count, meta):
    lane = lax.broadcasted_iota(jnp.int32, (SLOTS, SLOTS), 1)
    sub = lax.broadcasted_iota(jnp.int32, (SLOTS, SLOTS), 0)
    slot = lax.broadcasted_iota(jnp.int32, (SLOTS, 1), 0)
    across_slot = lax.broadcasted_iota(jnp.int32, (1, SLOTS), 1)

    def down(across):
        return jnp.sum(jnp.where(sub == lane, across, 0), axis=1, keepdims=True)

    rows, cols = coords_ref[0:1, :], coords_ref[1:2, :]
    rows_down, cols_down = down(rows), down(cols)
    live, live_down = across_slot < count, slot < count
    value = slot + rows_down * 256 + cols_down * 8192
    for at, (major, minor, major_down, minor_down) in enumerate(
        ((rows, cols, rows_down, cols_down), (cols, rows, cols_down, rows_down))
    ):
        key = jnp.where(live, major * TR + minor, TR * TR + across_slot)
        key_down = jnp.where(live_down, major_down * TR + minor_down, TR * TR + slot)
        rank = jnp.sum(jnp.where(key < key_down, 1, 0), axis=1, keepdims=True)
        meta[at : at + 1, 0:SLOTS] = jnp.sum(jnp.where(rank == lane, value, 0), axis=0, keepdims=True)
        upto = jnp.logical_and(major_down <= lane, live_down)
        meta[at + 2 : at + 3, 0:SLOTS] = jnp.sum(jnp.where(upto, 1, 0), axis=0, keepdims=True) - 1


def tile_sums(order, tiles, source, prefix, back, between=()):
    def place(slot):
        word = order[1 if back else 0, slot]
        index = word & 255
        row = lax.shift_right_logical(word, 8) & (TR - 1)
        col = lax.shift_right_logical(word, 13)
        return (index, col, row) if back else (index, row, col)

    def product(index, read):
        dims = (((0,), (0,)), ((), ())) if back else (((1,), (0,)), ((), ()))
        return lax.dot_general(tiles[index], source[read], dims, preferred_element_type=F32)

    def step(block, acc):
        start = block * UNROLL
        places = [place(start + u) for u in range(UNROLL)]
        before = place(jnp.maximum(start - 1, 0))[1]
        products = [product(index, read) for index, _, read in places]
        for u in range(UNROLL):
            write = places[u][1]
            acc = jnp.where(write == before, acc, 0.0) + products[u]
            prefix[start + u] = acc.astype(BF)
            before = write
        return acc

    steps, parts = SLOTS // UNROLL, len(between) + 1
    acc = jnp.zeros((T, H), F32)
    for n in range(parts):
        acc = lax.fori_loop(steps * n // parts, steps * (n + 1) // parts, step, acc)
        if n < len(between):
            between[n]()


def take(order, prefix, out, block, back):
    line = 3 if back else 2
    for u in range(2):
        r = 2 * block + u
        last = order[line, r]
        previous = jnp.where(r == 0, -1, order[line, jnp.maximum(r - 1, 0)])
        value = prefix[jnp.maximum(last, 0)]
        out[r] = jnp.where(last > previous, value, jnp.zeros_like(value))


def kernel(
    feats_hbm, weight_hbm, bias_hbm, cotangent_hbm, tiles_hbm, coords_hbm, counts,
    activations, weight_grad, bias_grad, feats_grad,
    feats_in, weight, bias, cotangent, coords,
    tiles, meta, order, p0, p1, f0, f1, s0, s1, u0, u1, xb0, xb1, xc0, xc1, xp0, xp1,
    zs0, zs1, zr0, zr1, own0, own1, agg, g0, g1,
    cr0, cr1, rs0, rs1, rr0, rr1, ws, wc, wy, ws2, wx, ws3, wl, ws4, wz, wout,
    local_sem, f_send, f_recv, fc_send, fc_recv, x_send, x_recv, z_send, z_recv,
    gz_send, gz_recv, gx_send, gx_recv, c_send, c_recv, r_send, r_recv, w_send, w_recv,
):
    row, col = lax.axis_index("row"), lax.axis_index("col")
    y, zl, core = lax.div(row, 4), lax.rem(lax.div(row, 2), 2), lax.rem(row, 2)
    zh, x = lax.div(col, 4), lax.rem(col, 4)
    side = 1 + 2 * core

    def row_at(dy, dz, dc):
        return (lax.rem(y + dy, 4) * 2 + lax.rem(zl + dz, 2)) * 2 + lax.rem(core + dc, 2)

    def col_at(dz, dx):
        return lax.rem(zh + dz, 4) * 4 + lax.rem(x + dx, 4)

    sibling = (row_at(0, 0, 1), col)
    ahead, behind = (row, col_at(0, side)), (row, col_at(0, 4 - side))
    chips = [(2, 1), (2, 0), (1, 1), (3, 1), (1, 0), (3, 0), (0, 1)]
    sends = []
    locals_ = []

    def send(src, dst, ssem, rsem, device):
        copy = pltpu.make_async_remote_copy(
            src_ref=src, dst_ref=dst, send_sem=ssem, recv_sem=rsem, device_id=device, device_id_type=MESH
        )
        copy.start()
        copy = Sent(copy)
        sends.append(copy)
        return copy

    def load(src, dst):
        copy = pltpu.make_async_copy(src, dst, local_sem.at[len(locals_)])
        copy.start()
        copy = Sent(copy)
        locals_.append(copy)
        return copy

    partners = [sibling]
    partners += [(row_at(dy, dz, 0), col) for dy, dz in chips]
    partners += [(row, col_at(0, d)) for d in range(1, 4)]
    partners += [(row, col_at(d, 0)) for d in range(1, 4)]
    barrier = pltpu.get_barrier_semaphore()
    for device in partners:
        pl.semaphore_signal(barrier, inc=1, device_id=device, device_id_type=MESH)
    load_feats = load(feats_hbm, feats_in)
    load_coords = load(coords_hbm, coords)
    load_tiles = load(tiles_hbm, tiles)
    load_dense = [load(weight_hbm, weight), load(bias_hbm, bias), load(cotangent_hbm, cotangent)]
    feats = (f0, f1)
    load_feats.wait()
    for h in range(2):
        feats[h][pl.ds(2 * row, 2)] = feats_in[:, h * H : (h + 1) * H].reshape(2, T, H)
    pl.semaphore_wait(barrier, len(partners))

    got = {}

    def send_features(h):
        mine = feats[h].at[pl.ds(2 * row, 2)]
        for n, (dy, dz) in enumerate(chips):
            got[h, n] = send(mine, mine, f_send.at[h, n], f_recv.at[h, n], (row_at(dy, dz, 0), col))
        got[h, 7] = send(mine, mine, fc_send.at[h, 7], fc_recv.at[h, 7], sibling)

    send_features(0)
    load_coords.wait()
    slot_order(coords, counts[0, 0], meta)
    load_order = load(meta, order)
    load_order.wait()
    load_tiles.wait()
    for copy in load_dense:
        copy.wait()

    sums = (s0, s1)
    prefix = (p0, p1)
    relay, combined, plain, summed = (u0, u1), (xb0, xb1), (xc0, xc1), (xp0, xp1)
    zsend = (zs0, zs1)
    zrecv = (zr0, zr1)
    own = (own0, own1)
    places = (2, 1, 3, 0)

    def gather_features(h, early=None):
        passed = []
        for at, n in enumerate((4, 5, 6, 2, 3, 1, 0)):
            dy, dz = chips[n]
            got[h, n].wait_recv()
            came = feats[h].at[pl.ds(2 * row_at(4 - dy, dz, 0), 2)]
            passed.append(send(came, came, fc_send.at[h, n], fc_recv.at[h, n], sibling))
            if early and at == 2:
                early()
        got[h, 7].wait_recv()
        for copy in passed:
            copy.wait_recv()

    xcopies = {}

    def send_sum(h, k, kind, src, dst, device):
        xcopies[h, k, kind] = send(src, dst, x_send.at[h, kind, k], x_recv.at[h, kind, k], device)

    def scatter_far(h, k):
        for kind, d, dst, device in ((0, 2, relay, ahead), (1, 4 - side, plain, behind)):
            block = col_at(k, d)
            take(order, prefix[h], sums[h], block, False)
            send_sum(h, k, kind, sums[h].at[pl.ds(2 * block, 2)], dst[h].at[k], device)

    def scatter_ahead(h, k):
        block = col_at(k, side)
        take(order, prefix[h], sums[h], block, False)
        xcopies[h, k, 0].wait_recv()
        mine = sums[h][pl.ds(2 * block, 2)]
        summed[h][k] = (mine.astype(F32) + relay[h][k].astype(F32)).astype(BF)
        send_sum(h, k, 2, summed[h].at[k], combined[h].at[k], ahead)

    zcopies = {}

    def scatter_z(h, k):
        block = col_at(k, 0)
        take(order, prefix[h], sums[h], block, False)
        xcopies[h, k, 1].wait_recv()
        xcopies[h, k, 2].wait_recv()
        total = sums[h][pl.ds(2 * block, 2)].astype(F32)
        total += plain[h][k].astype(F32) + combined[h][k].astype(F32)
        if k:
            zsend[h][k - 1] = total.astype(BF)
            zcopies[h, k] = send(
                zsend[h].at[k - 1], zrecv[h].at[k - 1], z_send.at[h, k - 1], z_recv.at[h, k - 1],
                (row, col_at(k, 0)),
            )
        else:
            own[h][...] = total

    def finish_aggregate(h):
        total = own[h][...]
        for k in range(1, 4):
            zcopies[h, k].wait_recv()
            total += zrecv[h][k - 1].astype(F32)
        agg[:, h * H : (h + 1) * H] = total.reshape(2 * T, H).astype(BF)

    units = [(h, k) for h in range(2) for k in (2, 1, 3, 0)]
    gather_features(0, lambda: send_features(1))
    tile_sums(order, tiles, f0, p0, False)
    scatter_far(*units[0])
    scatter_far(*units[1])
    gather_features(1)
    scatter_ahead(*units[0])
    scatter_far(*units[2])
    scatter_far(*units[3])
    tile_sums(order, tiles, f1, p1, False)
    for n in range(4, 12):
        if n < 8:
            scatter_far(*units[n])
        if n == 4:
            scatter_ahead(*units[1])
        if n < 10:
            scatter_ahead(*units[n - 2])
        if n >= 5:
            scatter_z(*units[n - 5])
    scatter_z(*units[7])
    finish_aggregate(0)
    finish_aggregate(1)

    pre = jnp.dot(agg[...], weight[...], preferred_element_type=F32) + bias[...]
    gate = jax.nn.sigmoid(pre)
    pre_grad = (cotangent[...].astype(F32) * gate * (1.0 + pre * (1.0 - gate))).astype(BF)
    agg_grad = lax.dot_general(
        pre_grad, weight[...], (((1,), (1,)), ((), ())), preferred_element_type=F32
    ).astype(BF)
    grads = (g0, g1)
    for h in range(2):
        grads[h][pl.ds(2 * col, 2)] = agg_grad[:, h * H : (h + 1) * H].reshape(2, T, H)

    gz = {}
    gx = {}

    def origin(k, d):
        return grads_at(col_at(4 - k if k else 0, d))

    def grads_at(block):
        return pl.ds(2 * block, 2)

    def spread(h, k):
        came = grads[h].at[origin(k, 0)]
        gx[h, k, 0] = send(came, came, gx_send.at[h, k, 0], gx_recv.at[h, k, 0], ahead)
        gx[h, k, 1] = send(came, came, gx_send.at[h, k, 1], gx_recv.at[h, k, 1], behind)

    def pass_on(h, k):
        gx[h, k, 0].wait_recv()
        came = grads[h].at[origin(k, 4 - side)]
        gx[h, k, 2] = send(came, came, gx_send.at[h, k, 2], gx_recv.at[h, k, 2], ahead)

    def spread_z(h, k):
        mine = grads[h].at[pl.ds(2 * col, 2)]
        gz[h, k] = send(mine, mine, gz_send.at[h, k - 1], gz_recv.at[h, k - 1], (row, col_at(k, 0)))

    def came_z(h, k):
        gz[h, k].wait_recv()
        spread(h, k)

    spread_z(0, 1)
    spread_z(0, 3)
    spread(0, 0)
    spread(1, 0)

    activations[...] = (pre * gate).astype(BF)
    part = lax.dot_general(agg[...], pre_grad, (((0,), (0,)), ((), ())), preferred_element_type=F32)
    bias_part = jnp.broadcast_to(jnp.sum(pre_grad.astype(F32), axis=0, keepdims=True), (8, F))
    for n in range(32):
        ws[n // 16, n // 4 % 4, n % 4, 0:8, :] = part[8 * n : 8 * n + 8, :]
        ws[n // 16, n // 4 % 4, n % 4, 8:16, :] = bias_part
    stage = {}
    wnext = [0]

    def wsend(name, src, dst, device):
        n = wnext[0]
        wnext[0] += 1
        stage.setdefault(name, []).append(send(src, dst, w_send.at[n], w_recv.at[n], device))

    def landed(name):
        for copy in stage[name]:
            copy.wait_recv()

    def along_y(d):
        return (row_at(d, 0, 0), col)

    def along_x(d):
        return (row, col_at(0, d))

    def w_core():
        wsend("core", ws.at[1 - core], wc, sibling)

    def w_y():
        landed("core")
        for a in range(4):
            ws2[a] = ws[core, a] + wc[a]
        for d in range(1, 4):
            wsend("y", ws2.at[lax.rem(y + d, 4)], wy.at[y], along_y(d))
        wy[y] = ws2[y]

    def w_x():
        landed("y")
        ws3[...] = ((wy[0] + wy[1]) + wy[2]) + wy[3]
        for d in range(1, 4):
            wsend("x", ws3.at[lax.rem(x + d, 4)], wx.at[x], along_x(d))
        wx[x] = ws3[x]

    def w_zl():
        landed("x")
        ws4[0] = ((wx[0] + wx[1]) + wx[2]) + wx[3]
        wsend("zl", ws4.at[0], wl, (row_at(0, 1, 0), col))

    def w_zh():
        landed("zl")
        ws4[1] = ws4[0] + wl[...]
        for d in range(1, 4):
            wsend("zh", ws4.at[1], wz.at[zh], (row, col_at(d, 0)))
        wz[zh] = ws4[1]

    def v_x():
        landed("zh")
        total = ((wz[0] + wz[1]) + wz[2]) + wz[3]
        bias_grad[...] = total[8:9, :]
        wout[core, y, x] = total[0:8, :]
        at = wout.at[core, y, x]
        for d in range(1, 4):
            wsend("vx", at, at, along_x(d))

    def v_y():
        landed("vx")
        at = wout.at[core, y]
        for d in range(1, 4):
            wsend("vy", at, at, along_y(d))

    def v_core():
        landed("vy")
        at = wout.at[core]
        wsend("vcore", at, at, sibling)

    def v_end():
        landed("vcore")
        weight_grad[...] = wout[...].reshape(F, F)

    def gathered(h):
        for k in range(4):
            for d in range(3):
                gx[h, k, d].wait_recv()

    cr = (cr0, cr1)
    rsend = (rs0, rs1)
    rrecv = (rr0, rr1)
    ccopies = {}
    rcopies = {}
    order_out = chips + [(0, 0)]

    def scatter_core(h):
        for n, (dy, dz) in enumerate(order_out):
            block = row_at(dy, dz, 1)
            take(order, prefix[h], sums[h], block, True)
            at = pl.ds(2 * block, 2)
            ccopies[h, n] = send(sums[h].at[at], cr[h].at[n], c_send.at[h, n], c_recv.at[h, n], sibling)

    def scatter_row(h, at=range(8)):
        for n in at:
            dy, dz = order_out[n]
            block = row_at(dy, dz, 0)
            take(order, prefix[h], sums[h], block, True)
            ccopies[h, n].wait_recv()
            total = sums[h][pl.ds(2 * block, 2)].astype(F32) + cr[h][n].astype(F32)
            if n < 7:
                rsend[h][n] = total.astype(BF)
                rcopies[h, n] = send(
                    rsend[h].at[n], rrecv[h].at[n], r_send.at[h, n], r_recv.at[h, n], (row_at(dy, dz, 0), col)
                )
            else:
                own[h][...] = total

    def finish_feats(h):
        total = own[h][...]
        for n in range(7):
            rcopies[h, n].wait_recv()
            total += rrecv[h][n].astype(F32)
        feats_grad[:, h * H : (h + 1) * H] = total.reshape(2 * T, H).astype(BF)

    w_core()
    pass_on(0, 0)
    came_z(0, 1)
    spread_z(0, 2)
    pass_on(1, 0)
    came_z(0, 3)
    pass_on(0, 1)
    w_y()
    came_z(0, 2)
    spread_z(1, 1)
    spread_z(1, 3)
    pass_on(0, 3)
    pass_on(0, 2)
    came_z(1, 1)
    spread_z(1, 2)
    came_z(1, 3)
    w_x()
    for copy in xcopies.values():
        copy.wait_send()
    gathered(0)

    def more_1():
        pass_on(1, 1)
        came_z(1, 2)

    def more_2():
        pass_on(1, 3)
        w_zl()

    tile_sums(order, tiles, g0, p0, True, (more_1, more_2))
    pass_on(1, 2)
    scatter_core(0)
    w_zh()
    gathered(1)

    def row_1():
        scatter_row(0, range(4))
        v_x()

    def row_2():
        scatter_row(0, range(4, 8))
        v_y()

    tile_sums(order, tiles, g1, p1, True, (row_1, row_2))
    scatter_core(1)
    scatter_row(1)
    v_core()
    finish_feats(0)
    finish_feats(1)
    v_end()
    for copy in sends:
        copy.wait_send()


def copy_out(*refs):
    for n in range(4):
        refs[n + 4][...] = refs[n][...]


def body(node_feats, weight, bias, cotangent, tiles, coords, counts):
    vmem = pl.BlockSpec(memory_space=pltpu.VMEM)
    hbm = pl.BlockSpec(memory_space=pltpu.HBM)
    half = (TR, T, H)
    dma = pltpu.SemaphoreType.DMA
    pair = lambda shape, dtype=BF: [pltpu.VMEM(shape, dtype)] * 2
    both = lambda shape: [dma(shape), dma(shape)]
    outs = (
        jax.ShapeDtypeStruct((2 * T, F), BF),
        jax.ShapeDtypeStruct((F, F), F32),
        jax.ShapeDtypeStruct((1, F), F32),
        jax.ShapeDtypeStruct((2 * T, F), BF),
    )
    results = pl.pallas_call(
        kernel,
        out_shape=outs,
        in_specs=[hbm] * 6 + [pl.BlockSpec(memory_space=pltpu.SMEM)],
        out_specs=(vmem, vmem, vmem, vmem),
        scratch_shapes=[
            pltpu.VMEM((2 * T, F), BF),
            pltpu.VMEM((F, F), BF),
            pltpu.VMEM((1, F), F32),
            pltpu.VMEM((2 * T, F), BF),
            pltpu.VMEM((2, SLOTS), jnp.int32),
            pltpu.VMEM((SLOTS, T, T), BF),
            pltpu.VMEM((8, 256), jnp.int32),
            pltpu.SMEM((8, 256), jnp.int32),
            *pair((SLOTS, T, H)),
            *pair(half),
            *pair(half),
            *pair((4, 2, T, H)),
            *pair((4, 2, T, H)),
            *pair((4, 2, T, H)),
            *pair((4, 2, T, H)),
            *pair((3, 2, T, H)),
            *pair((3, 2, T, H)),
            *pair((2, T, H), F32),
            pltpu.VMEM((2 * T, F), BF),
            *pair(half),
            *pair((8, 2, T, H)),
            *pair((7, 2, T, H)),
            *pair((7, 2, T, H)),
            pltpu.VMEM((2, 4, 4, 16, F), F32),
            pltpu.VMEM((4, 4, 16, F), F32),
            pltpu.VMEM((4, 4, 16, F), F32),
            pltpu.VMEM((4, 4, 16, F), F32),
            pltpu.VMEM((4, 16, F), F32),
            pltpu.VMEM((4, 16, F), F32),
            pltpu.VMEM((16, F), F32),
            pltpu.VMEM((2, 16, F), F32),
            pltpu.VMEM((4, 16, F), F32),
            pltpu.VMEM((2, 4, 4, 8, F), F32),
            dma((7,)),
            *both((2, 7)),
            *both((2, 8)),
            *both((2, 3, 4)),
            *both((2, 3)),
            *both((2, 3)),
            *both((2, 4, 3)),
            *both((2, 8)),
            *both((2, 7)),
            *both((18,)),
        ],
        compiler_params=pltpu.CompilerParams(
            collective_id=0, has_side_effects=True, vmem_limit_bytes=63 * 2**20
        ),
    )(node_feats, weight, bias.reshape(1, F), cotangent, tiles.reshape(SLOTS, T, T),
      coords.reshape(SLOTS, 2).T, counts)
    activations, weight_grad, bias_grad, feats_grad = pl.pallas_call(
        copy_out,
        out_shape=outs,
        in_specs=[vmem] * 4,
        out_specs=[vmem] * 4,
        compiler_params=pltpu.CompilerParams(vmem_limit_bytes=63 * 2**20),
    )(*results)
    return activations, weight_grad, bias_grad.reshape(F), feats_grad


def solution(mesh):
    return jax.shard_map(
        body,
        mesh=mesh,
        in_specs=(
            P(("col", "row"), None),
            P(),
            P(),
            P(("row", "col"), None),
            P("row", "col", None, None, None),
            P("row", "col", None, None),
            P("row", "col"),
        ),
        out_specs=(P(("row", "col"), None), P(), P(), P(("col", "row"), None)),
        check_vma=False,
    )
```

```python
import functools

import jax
import jax.numpy as jnp
from jax import lax
from jax.experimental import pallas as pl
from jax.experimental.pallas import tpu as pltpu
from jax.sharding import PartitionSpec as P

F = 256
H = 128
T = 128
SLOTS = 192
TR = 32
BF = jnp.bfloat16
F32 = jnp.float32
MESH = pl.DeviceIdType.MESH
UNROLL = 32
SUMS_X_STRAIGHT = frozenset(((1, 1), (1, 0)))
SUMS_Z_STRAIGHT = frozenset((1,))
GRADS_X_STRAIGHT = frozenset(())
GRADS_Z_STRAIGHT = frozenset(())


class Sent:
    def __init__(self, copy):
        self.copy, self.here, self.there = copy, False, False

    def wait_recv(self):
        if not self.here:
            self.copy.wait_recv()
        self.here = True

    def wait(self):
        if not self.here:
            self.copy.wait()
        self.here = True

    def wait_send(self):
        if not self.there:
            self.copy.wait_send()
        self.there = True


def slot_order(coords_ref, count, meta):
    lane = lax.broadcasted_iota(jnp.int32, (SLOTS, SLOTS), 1)
    sub = lax.broadcasted_iota(jnp.int32, (SLOTS, SLOTS), 0)
    slot = lax.broadcasted_iota(jnp.int32, (SLOTS, 1), 0)
    across_slot = lax.broadcasted_iota(jnp.int32, (1, SLOTS), 1)

    def down(across):
        return jnp.sum(jnp.where(sub == lane, across, 0), axis=1, keepdims=True)

    rows, cols = coords_ref[0:1, :], coords_ref[1:2, :]
    rows_down, cols_down = down(rows), down(cols)
    live, live_down = across_slot < count, slot < count
    value = slot + rows_down * 256 + cols_down * 8192
    for at, (major, minor, major_down, minor_down) in enumerate(
        ((rows, cols, rows_down, cols_down), (cols, rows, cols_down, rows_down))
    ):
        key = jnp.where(live, major * TR + minor, TR * TR + across_slot)
        key_down = jnp.where(live_down, major_down * TR + minor_down, TR * TR + slot)
        rank = jnp.sum(jnp.where(key < key_down, 1, 0), axis=1, keepdims=True)
        meta[at : at + 1, 0:SLOTS] = jnp.sum(jnp.where(rank == lane, value, 0), axis=0, keepdims=True)
        upto = jnp.logical_and(major_down <= lane, live_down)
        meta[at + 2 : at + 3, 0:SLOTS] = jnp.sum(jnp.where(upto, 1, 0), axis=0, keepdims=True) - 1


def tile_sums(order, tiles, source, prefix, back, between=()):
    def place(slot):
        word = order[1 if back else 0, slot]
        index = word & 255
        row = lax.shift_right_logical(word, 8) & (TR - 1)
        col = lax.shift_right_logical(word, 13)
        return (index, col, row) if back else (index, row, col)

    def product(index, read):
        left, right = (source[read], tiles[index]) if back else (tiles[index], source[read])
        return jnp.dot(left, right, preferred_element_type=F32)

    def step(block, acc):
        start = block * UNROLL
        places = [place(start + u) for u in range(UNROLL)]
        before = place(jnp.maximum(start - 1, 0))[1]
        products = [product(index, read) for index, _, read in places]
        for u in range(UNROLL):
            write = places[u][1]
            acc = jnp.where(write == before, acc, 0.0) + products[u]
            prefix[start + u] = acc.astype(BF)
            before = write
        return acc

    steps, parts = SLOTS // UNROLL, len(between) + 1
    acc = jnp.zeros((T, H), F32)
    for n in range(parts):
        acc = lax.fori_loop(steps * n // parts, steps * (n + 1) // parts, step, acc)
        if n < len(between):
            between[n]()


def take(order, prefix, out, block, back):
    line = 3 if back else 2
    for u in range(2):
        r = 2 * block + u
        last = order[line, r]
        previous = jnp.where(r == 0, -1, order[line, jnp.maximum(r - 1, 0)])
        value = prefix[jnp.maximum(last, 0)]
        out[r] = jnp.where(last > previous, value, jnp.zeros_like(value))


def kernel(
    feats_hbm, weight_hbm, bias_hbm, cotangent_hbm, tiles_hbm, coords_hbm, counts,
    activations, weight_grad, bias_grad, feats_grad,
    feats_in, weight, bias, cotangent, coords,
    tiles, meta, order, p0, p1, f0, f1, s0, s1, u0, u1, xb0, xb1, xc0, xc1, xp0, xp1,
    zs0, zs1, zr0, zr1, own0, own1, agg, g0, g1,
    cr0, cr1, rs0, rs1, rr0, rr1, ws, wc, wy, ws2, wx, ws3, wl, ws4, wz, wout,
    local_sem, f_send, f_recv, fc_send, fc_recv, x_send, x_recv, z_send, z_recv,
    gz_send, gz_recv, gx_send, gx_recv, c_send, c_recv, r_send, r_recv, w_send, w_recv,
):
    row, col = lax.axis_index("row"), lax.axis_index("col")
    y, zl, core = lax.div(row, 4), lax.rem(lax.div(row, 2), 2), lax.rem(row, 2)
    zh, x = lax.div(col, 4), lax.rem(col, 4)
    side = 1 + 2 * core

    def row_at(dy, dz, dc):
        return (lax.rem(y + dy, 4) * 2 + lax.rem(zl + dz, 2)) * 2 + lax.rem(core + dc, 2)

    def col_at(dz, dx):
        return lax.rem(zh + dz, 4) * 4 + lax.rem(x + dx, 4)

    sibling = (row_at(0, 0, 1), col)
    ahead, behind = (row, col_at(0, side)), (row, col_at(0, 4 - side))
    chips = [(2, 1), (2, 0), (1, 1), (3, 1), (1, 0), (3, 0), (0, 1)]
    sends = []
    locals_ = []

    def send(src, dst, ssem, rsem, device):
        copy = pltpu.make_async_remote_copy(
            src_ref=src, dst_ref=dst, send_sem=ssem, recv_sem=rsem, device_id=device, device_id_type=MESH
        )
        copy.start()
        copy = Sent(copy)
        sends.append(copy)
        return copy

    def load(src, dst):
        copy = pltpu.make_async_copy(src, dst, local_sem.at[len(locals_)])
        copy.start()
        copy = Sent(copy)
        locals_.append(copy)
        return copy

    partners = [sibling]
    partners += [(row_at(dy, dz, 0), col) for dy, dz in chips]
    partners += [(row, col_at(0, d)) for d in range(1, 4)]
    partners += [(row, col_at(d, 0)) for d in range(1, 4)]
    barrier = pltpu.get_barrier_semaphore()
    for device in partners:
        pl.semaphore_signal(barrier, inc=1, device_id=device, device_id_type=MESH)
    load_feats = load(feats_hbm, feats_in)
    load_coords = load(coords_hbm, coords)
    load_tiles = load(tiles_hbm, tiles)
    load_dense = [load(weight_hbm, weight), load(bias_hbm, bias), load(cotangent_hbm, cotangent)]
    feats = (f0, f1)
    load_feats.wait()
    for h in range(2):
        feats[h][pl.ds(2 * row, 2)] = feats_in[:, h * H : (h + 1) * H].reshape(2, T, H)
    pl.semaphore_wait(barrier, len(partners))

    got = {}

    def send_features(h):
        mine = feats[h].at[pl.ds(2 * row, 2)]
        for n, (dy, dz) in enumerate(chips):
            got[h, n] = send(mine, mine, f_send.at[h, n], f_recv.at[h, n], (row_at(dy, dz, 0), col))
        got[h, 7] = send(mine, mine, fc_send.at[h, 7], fc_recv.at[h, 7], sibling)

    send_features(0)
    load_coords.wait()
    slot_order(coords, counts[0, 0], meta)
    load_order = load(meta, order)
    load_order.wait()
    load_tiles.wait()
    for copy in load_dense:
        copy.wait()

    sums = (s0, s1)
    prefix = (p0, p1)
    relay, combined, plain, summed = (u0, u1), (xb0, xb1), (xc0, xc1), (xp0, xp1)
    zsend = (zs0, zs1)
    zrecv = (zr0, zr1)
    own = (own0, own1)
    away = (0, side, 2, 4 - side)
    ahead_z, behind_z = (row, col_at(side, 0)), (row, col_at(4 - side, 0))
    far, far_z = (row, col_at(0, 2)), (row, col_at(2, 0))

    def gather_features(h, early=None):
        passed = []
        for at, n in enumerate((4, 5, 6, 2, 3, 1, 0)):
            dy, dz = chips[n]
            got[h, n].wait_recv()
            came = feats[h].at[pl.ds(2 * row_at(4 - dy, dz, 0), 2)]
            passed.append(send(came, came, fc_send.at[h, n], fc_recv.at[h, n], sibling))
            if early and at == 2:
                early()
        got[h, 7].wait_recv()
        for copy in passed:
            copy.wait_recv()

    xcopies = {}

    def send_sum(h, k, kind, src, dst, device):
        xcopies[h, k, kind] = send(src, dst, x_send.at[h, kind, k], x_recv.at[h, kind, k], device)

    def scatter_far(h, k):
        for kind, d, dst, device in ((0, 2, relay, ahead), (1, 4 - side, plain, behind)):
            block = col_at(away[k], d)
            take(order, prefix[h], sums[h], block, False)
            if kind == 0 and (h, k) in SUMS_X_STRAIGHT:
                device = far
            send_sum(h, k, kind, sums[h].at[pl.ds(2 * block, 2)], dst[h].at[k], device)

    def scatter_ahead(h, k):
        block = col_at(away[k], side)
        take(order, prefix[h], sums[h], block, False)
        mine = pl.ds(2 * block, 2)
        if (h, k) in SUMS_X_STRAIGHT:
            send_sum(h, k, 2, sums[h].at[mine], combined[h].at[k], ahead)
            return
        xcopies[h, k, 0].wait_recv()
        summed[h][k] = (sums[h][mine].astype(F32) + relay[h][k].astype(F32)).astype(BF)
        send_sum(h, k, 2, summed[h].at[k], combined[h].at[k], ahead)

    zcopies = {}

    def scatter_z(h, k):
        block = col_at(away[k], 0)
        take(order, prefix[h], sums[h], block, False)
        xcopies[h, k, 1].wait_recv()
        xcopies[h, k, 2].wait_recv()
        total = sums[h][pl.ds(2 * block, 2)].astype(F32)
        total += plain[h][k].astype(F32) + combined[h][k].astype(F32)
        if (h, k) in SUMS_X_STRAIGHT:
            xcopies[h, k, 0].wait_recv()
            total += relay[h][k].astype(F32)
        if k == 1 and h not in SUMS_Z_STRAIGHT:
            zcopies[h, 2].wait_recv()
            total += zrecv[h][1].astype(F32)
        if k:
            zsend[h][k - 1] = total.astype(BF)
            zcopies[h, k] = send(
                zsend[h].at[k - 1], zrecv[h].at[k - 1], z_send.at[h, k - 1], z_recv.at[h, k - 1],
                (ahead_z, far_z if h in SUMS_Z_STRAIGHT else ahead_z, behind_z)[k - 1],
            )
        else:
            own[h][...] = total

    def finish_aggregate(h):
        total = own[h][...]
        for k in (3, 1, 2) if h in SUMS_Z_STRAIGHT else (3, 1):
            zcopies[h, k].wait_recv()
            total += zrecv[h][k - 1].astype(F32)
        agg[:, h * H : (h + 1) * H] = total.reshape(2 * T, H).astype(BF)

    gather_features(0, lambda: send_features(1))
    tile_sums(order, tiles, f0, p0, False)
    scatter_far(0, 2)
    scatter_far(0, 3)
    scatter_ahead(0, 2)
    gather_features(1)
    scatter_far(0, 1)
    scatter_far(0, 0)
    scatter_ahead(0, 3)
    tile_sums(order, tiles, f1, p1, False, (lambda: scatter_z(0, 2),))
    scatter_far(1, 2)
    scatter_ahead(0, 1)
    scatter_ahead(0, 0)
    scatter_z(0, 3)
    scatter_far(1, 3)
    scatter_z(0, 1)
    scatter_far(1, 1)
    scatter_ahead(1, 2)
    scatter_z(0, 0)
    scatter_ahead(1, 3)
    scatter_far(1, 0)
    scatter_z(1, 2)
    scatter_ahead(1, 1)
    scatter_z(1, 3)
    scatter_ahead(1, 0)
    scatter_z(1, 1)
    scatter_z(1, 0)
    finish_aggregate(0)
    finish_aggregate(1)

    pre = jnp.dot(agg[...], weight[...], preferred_element_type=F32) + bias[...]
    gate = jax.nn.sigmoid(pre)
    pre_grad = (cotangent[...].astype(F32) * gate * (1.0 + pre * (1.0 - gate))).astype(BF)
    grads = (g0, g1)
    for h in range(2):
        agg_grad = lax.dot_general(
            weight[h * H : (h + 1) * H, :], pre_grad, (((1,), (1,)), ((), ())), preferred_element_type=F32
        ).astype(BF)
        for t in range(2):
            grads[h][2 * col + t] = agg_grad[:, t * T : (t + 1) * T]

    gz = {}
    gx = {}

    def origin(k, d):
        return pl.ds(2 * col_at((0, 4 - side, 2, side)[k], d), 2)

    def spread(h, k):
        came = grads[h].at[origin(k, 0)]
        gx[h, k, 0] = send(came, came, gx_send.at[h, k, 0], gx_recv.at[h, k, 0], ahead)
        gx[h, k, 1] = send(came, came, gx_send.at[h, k, 1], gx_recv.at[h, k, 1], behind)
        if (h, k) in GRADS_X_STRAIGHT:
            gx[h, k, 2] = send(came, came, gx_send.at[h, k, 2], gx_recv.at[h, k, 2], far)

    def pass_on(h, k):
        if (h, k) in GRADS_X_STRAIGHT:
            return
        gx[h, k, 0].wait_recv()
        came = grads[h].at[origin(k, 4 - side)]
        gx[h, k, 2] = send(came, came, gx_send.at[h, k, 2], gx_recv.at[h, k, 2], ahead)

    def spread_z(h, k):
        straight = h in GRADS_Z_STRAIGHT
        block = grads[h].at[origin(1 if k == 2 and not straight else 0, 0)]
        device = (ahead_z, far_z if straight else ahead_z, behind_z)[k - 1]
        gz[h, k] = send(block, block, gz_send.at[h, k - 1], gz_recv.at[h, k - 1], device)

    def came_z(h, k):
        gz[h, k].wait_recv()
        if k == 1 and h not in GRADS_Z_STRAIGHT:
            spread_z(h, 2)
        spread(h, k)

    spread_z(0, 1)
    spread_z(0, 3)
    if 0 in GRADS_Z_STRAIGHT:
        spread_z(0, 2)
    spread(0, 0)
    spread(1, 0)

    activations[...] = (pre * gate).astype(BF)
    part = lax.dot_general(agg[...], pre_grad, (((0,), (0,)), ((), ())), preferred_element_type=F32)
    bias_part = jnp.broadcast_to(jnp.sum(pre_grad.astype(F32), axis=0, keepdims=True), (8, F))
    for n in range(32):
        ws[n // 16, n // 4 % 4, n % 4, 0:8, :] = part[8 * n : 8 * n + 8, :]
        ws[n // 16, n // 4 % 4, n % 4, 8:16, :] = bias_part
    stage = {}
    wnext = [0]

    def wsend(name, src, dst, device):
        n = wnext[0]
        wnext[0] += 1
        stage.setdefault(name, []).append(send(src, dst, w_send.at[n], w_recv.at[n], device))

    def landed(name):
        for copy in stage[name]:
            copy.wait_recv()

    def along_y(d):
        return (row_at(d, 0, 0), col)

    def along_x(d):
        return (row, col_at(0, d))

    def w_core():
        wsend("core", ws.at[1 - core], wc, sibling)

    def w_y():
        landed("core")
        for a in range(4):
            ws2[a] = ws[core, a] + wc[a]
        for d in range(1, 4):
            wsend("y", ws2.at[lax.rem(y + d, 4)], wy.at[y], along_y(d))
        wy[y] = ws2[y]

    def w_x():
        landed("y")
        ws3[...] = ((wy[0] + wy[1]) + wy[2]) + wy[3]
        for d in range(1, 4):
            wsend("x", ws3.at[lax.rem(x + d, 4)], wx.at[x], along_x(d))
        wx[x] = ws3[x]

    def w_zl():
        landed("x")
        ws4[0] = ((wx[0] + wx[1]) + wx[2]) + wx[3]
        wsend("zl", ws4.at[0], wl, (row_at(0, 1, 0), col))

    def w_zh():
        landed("zl")
        ws4[1] = ws4[0] + wl[...]
        for d in range(1, 4):
            wsend("zh", ws4.at[1], wz.at[zh], (row, col_at(d, 0)))
        wz[zh] = ws4[1]

    def v_x():
        landed("zh")
        total = ((wz[0] + wz[1]) + wz[2]) + wz[3]
        bias_grad[...] = total[8:9, :]
        wout[core, y, x] = total[0:8, :]
        at = wout.at[core, y, x]
        for d in range(1, 4):
            wsend("vx", at, at, along_x(d))

    def v_y():
        landed("vx")
        at = wout.at[core, y]
        for d in range(1, 4):
            wsend("vy", at, at, along_y(d))

    def v_core():
        landed("vy")
        at = wout.at[core]
        wsend("vcore", at, at, sibling)

    def v_end():
        landed("vcore")
        weight_grad[...] = wout[...].reshape(F, F)

    def gathered(h):
        for k in range(4):
            for d in range(3):
                gx[h, k, d].wait_recv()

    cr = (cr0, cr1)
    rsend = (rs0, rs1)
    rrecv = (rr0, rr1)
    ccopies = {}
    rcopies = {}
    order_out = chips + [(0, 0)]

    def scatter_core(h):
        for n, (dy, dz) in enumerate(order_out):
            block = row_at(dy, dz, 1)
            take(order, prefix[h], sums[h], block, True)
            at = pl.ds(2 * block, 2)
            ccopies[h, n] = send(sums[h].at[at], cr[h].at[n], c_send.at[h, n], c_recv.at[h, n], sibling)

    def scatter_row(h, at=range(8)):
        for n in at:
            dy, dz = order_out[n]
            block = row_at(dy, dz, 0)
            take(order, prefix[h], sums[h], block, True)
            ccopies[h, n].wait_recv()
            total = sums[h][pl.ds(2 * block, 2)].astype(F32) + cr[h][n].astype(F32)
            if n < 7:
                rsend[h][n] = total.astype(BF)
                rcopies[h, n] = send(
                    rsend[h].at[n], rrecv[h].at[n], r_send.at[h, n], r_recv.at[h, n], (row_at(dy, dz, 0), col)
                )
            else:
                own[h][...] = total

    def finish_feats(h):
        total = own[h][...]
        for n in range(7):
            rcopies[h, n].wait_recv()
            total += rrecv[h][n].astype(F32)
        for t in range(2):
            feats_grad[t * T : (t + 1) * T, h * H : (h + 1) * H] = total[t].T.astype(BF)

    w_core()
    pass_on(0, 0)
    came_z(0, 1)
    came_z(0, 3)
    pass_on(1, 0)
    spread_z(1, 1)
    spread_z(1, 3)
    if 1 in GRADS_Z_STRAIGHT:
        spread_z(1, 2)
    pass_on(0, 1)
    came_z(0, 2)
    pass_on(0, 3)
    w_y()
    came_z(1, 1)
    pass_on(0, 2)
    came_z(1, 3)
    w_x()
    for copy in xcopies.values():
        copy.wait_send()
    gathered(0)

    def more_1():
        pass_on(1, 1)
        came_z(1, 2)

    def more_2():
        pass_on(1, 3)
        w_zl()

    tile_sums(order, tiles, g0, p0, True, (more_1, more_2))
    pass_on(1, 2)
    scatter_core(0)
    w_zh()
    gathered(1)

    def row_1():
        scatter_row(0, range(4))
        v_x()

    def row_2():
        scatter_row(0, range(4, 8))
        v_y()

    tile_sums(order, tiles, g1, p1, True, (row_1, row_2))
    scatter_core(1)
    scatter_row(1)
    v_core()
    finish_feats(0)
    finish_feats(1)
    v_end()
    for copy in sends:
        copy.wait_send()


def copy_out(*refs):
    for n in range(4):
        refs[n + 4][...] = refs[n][...]


def body(node_feats, weight, bias, cotangent, tiles, coords, counts):
    vmem = pl.BlockSpec(memory_space=pltpu.VMEM)
    hbm = pl.BlockSpec(memory_space=pltpu.HBM)
    half = (TR, T, H)
    dma = pltpu.SemaphoreType.DMA
    pair = lambda shape, dtype=BF: [pltpu.VMEM(shape, dtype)] * 2
    both = lambda shape: [dma(shape), dma(shape)]
    outs = (
        jax.ShapeDtypeStruct((2 * T, F), BF),
        jax.ShapeDtypeStruct((F, F), F32),
        jax.ShapeDtypeStruct((1, F), F32),
        jax.ShapeDtypeStruct((2 * T, F), BF),
    )
    results = pl.pallas_call(
        kernel,
        out_shape=outs,
        in_specs=[hbm] * 6 + [pl.BlockSpec(memory_space=pltpu.SMEM)],
        out_specs=(vmem, vmem, vmem, vmem),
        scratch_shapes=[
            pltpu.VMEM((2 * T, F), BF),
            pltpu.VMEM((F, F), BF),
            pltpu.VMEM((1, F), F32),
            pltpu.VMEM((2 * T, F), BF),
            pltpu.VMEM((2, SLOTS), jnp.int32),
            pltpu.VMEM((SLOTS, T, T), BF),
            pltpu.VMEM((8, 256), jnp.int32),
            pltpu.SMEM((8, 256), jnp.int32),
            *pair((SLOTS, T, H)),
            *pair(half),
            *pair(half),
            *pair((4, 2, T, H)),
            *pair((4, 2, T, H)),
            *pair((4, 2, T, H)),
            *pair((4, 2, T, H)),
            *pair((3, 2, T, H)),
            *pair((3, 2, T, H)),
            *pair((2, T, H), F32),
            pltpu.VMEM((2 * T, F), BF),
            *pair(half),
            *pair((8, 2, T, H)),
            *pair((7, 2, T, H)),
            *pair((7, 2, T, H)),
            pltpu.VMEM((2, 4, 4, 16, F), F32),
            pltpu.VMEM((4, 4, 16, F), F32),
            pltpu.VMEM((4, 4, 16, F), F32),
            pltpu.VMEM((4, 4, 16, F), F32),
            pltpu.VMEM((4, 16, F), F32),
            pltpu.VMEM((4, 16, F), F32),
            pltpu.VMEM((16, F), F32),
            pltpu.VMEM((2, 16, F), F32),
            pltpu.VMEM((4, 16, F), F32),
            pltpu.VMEM((2, 4, 4, 8, F), F32),
            dma((7,)),
            *both((2, 7)),
            *both((2, 8)),
            *both((2, 3, 4)),
            *both((2, 3)),
            *both((2, 3)),
            *both((2, 4, 3)),
            *both((2, 8)),
            *both((2, 7)),
            *both((18,)),
        ],
        compiler_params=pltpu.CompilerParams(
            collective_id=0, has_side_effects=True, vmem_limit_bytes=63 * 2**20
        ),
    )(node_feats, weight, bias.reshape(1, F), cotangent, tiles.reshape(SLOTS, T, T),
      coords.reshape(SLOTS, 2).T, counts)
    activations, weight_grad, bias_grad, feats_grad = pl.pallas_call(
        copy_out,
        out_shape=outs,
        in_specs=[vmem] * 4,
        out_specs=[vmem] * 4,
        compiler_params=pltpu.CompilerParams(vmem_limit_bytes=63 * 2**20),
    )(*results)
    return activations, weight_grad, bias_grad.reshape(F), feats_grad


def solution(mesh):
    return jax.shard_map(
        body,
        mesh=mesh,
        in_specs=(
            P(("col", "row"), None),
            P(),
            P(),
            P(("row", "col"), None),
            P("row", "col", None, None, None),
            P("row", "col", None, None),
            P("row", "col"),
        ),
        out_specs=(P(("row", "col"), None), P(), P(), P(("col", "row"), None)),
        check_vma=False,
    )
```

```python
import functools

import jax
import jax.numpy as jnp
from jax import lax
from jax.experimental import pallas as pl
from jax.experimental.pallas import tpu as pltpu
from jax.sharding import PartitionSpec as P

F = 256
H = 128
T = 128
SLOTS = 192
TR = 32
BF = jnp.bfloat16
F32 = jnp.float32
MESH = pl.DeviceIdType.MESH
UNROLL = 32
SUMS_X_STRAIGHT = frozenset(((1, 1), (1, 0)))
SUMS_Z_STRAIGHT = frozenset((1,))
GRADS_X_STRAIGHT = frozenset(())
GRADS_Z_STRAIGHT = frozenset(())


class Sent:
    def __init__(self, copy):
        self.copy, self.here, self.there = copy, False, False

    def wait_recv(self):
        if not self.here:
            self.copy.wait_recv()
        self.here = True

    def wait(self):
        if not self.here:
            self.copy.wait()
        self.here = True

    def wait_send(self):
        if not self.there:
            self.copy.wait_send()
        self.there = True


def slot_order(coords_ref, count, meta):
    lane = lax.broadcasted_iota(jnp.int32, (SLOTS, SLOTS), 1)
    sub = lax.broadcasted_iota(jnp.int32, (SLOTS, SLOTS), 0)
    slot = lax.broadcasted_iota(jnp.int32, (SLOTS, 1), 0)
    across_slot = lax.broadcasted_iota(jnp.int32, (1, SLOTS), 1)

    def down(across):
        return jnp.sum(jnp.where(sub == lane, across, 0), axis=1, keepdims=True)

    rows, cols = coords_ref[0:1, :], coords_ref[1:2, :]
    rows_down, cols_down = down(rows), down(cols)
    live, live_down = across_slot < count, slot < count
    value = slot + rows_down * 256 + cols_down * 8192
    for at, (major, minor, major_down, minor_down) in enumerate(
        ((rows, cols, rows_down, cols_down), (cols, rows, cols_down, rows_down))
    ):
        key = jnp.where(live, major * TR + minor, TR * TR + across_slot)
        key_down = jnp.where(live_down, major_down * TR + minor_down, TR * TR + slot)
        rank = jnp.sum(jnp.where(key < key_down, 1, 0), axis=1, keepdims=True)
        meta[at : at + 1, 0:SLOTS] = jnp.sum(jnp.where(rank == lane, value, 0), axis=0, keepdims=True)
        upto = jnp.logical_and(major_down <= lane, live_down)
        meta[at + 2 : at + 3, 0:SLOTS] = jnp.sum(jnp.where(upto, 1, 0), axis=0, keepdims=True) - 1


def tile_sums(order, tiles, source, prefix, back, between=()):
    def place(slot):
        word = order[1 if back else 0, slot]
        index = word & 255
        row = lax.shift_right_logical(word, 8) & (TR - 1)
        col = lax.shift_right_logical(word, 13)
        return (index, col, row) if back else (index, row, col)

    def product(index, read):
        left, right = (source[read], tiles[index]) if back else (tiles[index], source[read])
        return jnp.dot(left, right, preferred_element_type=F32)

    def step(block, acc):
        start = block * UNROLL
        places = [place(start + u) for u in range(UNROLL)]
        before = place(jnp.maximum(start - 1, 0))[1]
        products = [product(index, read) for index, _, read in places]
        for u in range(UNROLL):
            write = places[u][1]
            acc = jnp.where(write == before, acc, 0.0) + products[u]
            prefix[start + u] = acc.astype(BF)
            before = write
        return acc

    steps, parts = SLOTS // UNROLL, len(between) + 1
    acc = jnp.zeros((T, H), F32)
    for n in range(parts):
        acc = lax.fori_loop(steps * n // parts, steps * (n + 1) // parts, step, acc)
        if n < len(between):
            between[n]()


def take(order, prefix, out, block, back):
    line = 3 if back else 2
    for u in range(2):
        r = 2 * block + u
        last = order[line, r]
        previous = jnp.where(r == 0, -1, order[line, jnp.maximum(r - 1, 0)])
        value = prefix[jnp.maximum(last, 0)]
        out[r] = jnp.where(last > previous, value, jnp.zeros_like(value))


def kernel(
    feats_hbm, weight_hbm, bias_hbm, cotangent_hbm, tiles_hbm, coords_hbm, counts,
    activations, weight_grad, bias_grad, feats_grad,
    feats_in, weight, bias, cotangent, coords,
    tiles, meta, order, p0, p1, f0, f1, s0, s1, u0, u1, xb0, xb1, xc0, xc1, xp0, xp1,
    zs0, zs1, zr0, zr1, own0, own1, agg, g0, g1,
    cr0, cr1, rs0, rs1, rr0, rr1, ws, wc, wy, ws2, wx, ws3, wl, ws4, wz, wout,
    local_sem, f_send, f_recv, fc_send, fc_recv, x_send, x_recv, z_send, z_recv,
    gz_send, gz_recv, gx_send, gx_recv, c_send, c_recv, r_send, r_recv, w_send, w_recv,
):
    row, col = lax.axis_index("row"), lax.axis_index("col")
    y, zl, core = lax.div(row, 4), lax.rem(lax.div(row, 2), 2), lax.rem(row, 2)
    zh, x = lax.div(col, 4), lax.rem(col, 4)
    side = 1 + 2 * core

    def row_at(dy, dz, dc):
        return (lax.rem(y + dy, 4) * 2 + lax.rem(zl + dz, 2)) * 2 + lax.rem(core + dc, 2)

    def col_at(dz, dx):
        return lax.rem(zh + dz, 4) * 4 + lax.rem(x + dx, 4)

    sibling = (row_at(0, 0, 1), col)
    ahead, behind = (row, col_at(0, side)), (row, col_at(0, 4 - side))
    chips = [(2, 1), (2, 0), (1, 1), (3, 1), (1, 0), (3, 0), (0, 1)]
    sends = []
    locals_ = []

    def send(src, dst, ssem, rsem, device):
        copy = pltpu.make_async_remote_copy(
            src_ref=src, dst_ref=dst, send_sem=ssem, recv_sem=rsem, device_id=device, device_id_type=MESH
        )
        copy.start()
        copy = Sent(copy)
        sends.append(copy)
        return copy

    def load(src, dst):
        copy = pltpu.make_async_copy(src, dst, local_sem.at[len(locals_)])
        copy.start()
        copy = Sent(copy)
        locals_.append(copy)
        return copy

    partners = [sibling]
    partners += [(row_at(dy, dz, 0), col) for dy, dz in chips]
    partners += [(row, col_at(0, d)) for d in range(1, 4)]
    partners += [(row, col_at(d, 0)) for d in range(1, 4)]
    barrier = pltpu.get_barrier_semaphore()
    for device in partners:
        pl.semaphore_signal(barrier, inc=1, device_id=device, device_id_type=MESH)
    load_feats = load(feats_hbm, feats_in)
    load_coords = load(coords_hbm, coords)
    load_tiles = load(tiles_hbm, tiles)
    load_dense = [load(weight_hbm, weight), load(bias_hbm, bias), load(cotangent_hbm, cotangent)]
    feats = (f0, f1)
    load_feats.wait()
    for h in range(2):
        feats[h][pl.ds(2 * row, 2)] = feats_in[:, h * H : (h + 1) * H].reshape(2, T, H)
    pl.semaphore_wait(barrier, len(partners))

    got = {}

    def send_features(h):
        mine = feats[h].at[pl.ds(2 * row, 2)]
        for n, (dy, dz) in enumerate(chips):
            got[h, n] = send(mine, mine, f_send.at[h, n], f_recv.at[h, n], (row_at(dy, dz, 0), col))
        got[h, 7] = send(mine, mine, fc_send.at[h, 7], fc_recv.at[h, 7], sibling)

    send_features(0)
    load_coords.wait()
    slot_order(coords, counts[0, 0], meta)
    load_order = load(meta, order)
    load_order.wait()
    load_tiles.wait()
    for copy in load_dense:
        copy.wait()

    sums = (s0, s1)
    prefix = (p0, p1)
    relay, combined, plain, summed = (u0, u1), (xb0, xb1), (xc0, xc1), (xp0, xp1)
    zsend = (zs0, zs1)
    zrecv = (zr0, zr1)
    own = (own0, own1)
    away = (0, side, 2, 4 - side)
    ahead_z, behind_z = (row, col_at(side, 0)), (row, col_at(4 - side, 0))
    far, far_z = (row, col_at(0, 2)), (row, col_at(2, 0))

    def gather_features(h, early=None):
        passed = []
        for at, n in enumerate((4, 5, 6, 2, 3, 1, 0)):
            dy, dz = chips[n]
            got[h, n].wait_recv()
            came = feats[h].at[pl.ds(2 * row_at(4 - dy, dz, 0), 2)]
            passed.append(send(came, came, fc_send.at[h, n], fc_recv.at[h, n], sibling))
            if early and at == 2:
                early()
        got[h, 7].wait_recv()
        for copy in passed:
            copy.wait_recv()

    xcopies = {}

    def send_sum(h, k, kind, src, dst, device):
        xcopies[h, k, kind] = send(src, dst, x_send.at[h, kind, k], x_recv.at[h, kind, k], device)

    def scatter_far(h, k):
        for kind, d, dst, device in ((0, 2, relay, ahead), (1, 4 - side, plain, behind)):
            block = col_at(away[k], d)
            take(order, prefix[h], sums[h], block, False)
            if kind == 0 and (h, k) in SUMS_X_STRAIGHT:
                device = far
            send_sum(h, k, kind, sums[h].at[pl.ds(2 * block, 2)], dst[h].at[k], device)

    def scatter_ahead(h, k):
        block = col_at(away[k], side)
        take(order, prefix[h], sums[h], block, False)
        mine = pl.ds(2 * block, 2)
        if (h, k) in SUMS_X_STRAIGHT:
            send_sum(h, k, 2, sums[h].at[mine], combined[h].at[k], ahead)
            return
        xcopies[h, k, 0].wait_recv()
        summed[h][k] = (sums[h][mine].astype(F32) + relay[h][k].astype(F32)).astype(BF)
        send_sum(h, k, 2, summed[h].at[k], combined[h].at[k], ahead)

    zcopies = {}

    def scatter_z(h, k):
        block = col_at(away[k], 0)
        take(order, prefix[h], sums[h], block, False)
        xcopies[h, k, 1].wait_recv()
        xcopies[h, k, 2].wait_recv()
        total = sums[h][pl.ds(2 * block, 2)].astype(F32)
        total += plain[h][k].astype(F32) + combined[h][k].astype(F32)
        if (h, k) in SUMS_X_STRAIGHT:
            xcopies[h, k, 0].wait_recv()
            total += relay[h][k].astype(F32)
        if k == 1 and h not in SUMS_Z_STRAIGHT:
            zcopies[h, 2].wait_recv()
            total += zrecv[h][1].astype(F32)
        if k:
            zsend[h][k - 1] = total.astype(BF)
            zcopies[h, k] = send(
                zsend[h].at[k - 1], zrecv[h].at[k - 1], z_send.at[h, k - 1], z_recv.at[h, k - 1],
                (ahead_z, far_z if h in SUMS_Z_STRAIGHT else ahead_z, behind_z)[k - 1],
            )
        else:
            own[h][...] = total

    def finish_aggregate(h):
        total = own[h][...]
        for k in (3, 1, 2) if h in SUMS_Z_STRAIGHT else (3, 1):
            zcopies[h, k].wait_recv()
            total += zrecv[h][k - 1].astype(F32)
        agg[:, h * H : (h + 1) * H] = total.reshape(2 * T, H).astype(BF)

    gather_features(0, lambda: send_features(1))
    tile_sums(order, tiles, f0, p0, False)
    scatter_far(0, 2)
    scatter_far(0, 3)
    scatter_ahead(0, 2)
    gather_features(1)
    scatter_far(0, 1)
    scatter_far(0, 0)
    scatter_ahead(0, 3)
    tile_sums(order, tiles, f1, p1, False, (lambda: scatter_z(0, 2),))
    scatter_far(1, 2)
    scatter_ahead(0, 1)
    scatter_ahead(0, 0)
    scatter_z(0, 3)
    scatter_far(1, 3)
    scatter_z(0, 1)
    scatter_far(1, 1)
    scatter_ahead(1, 2)
    scatter_z(0, 0)
    scatter_ahead(1, 3)
    scatter_far(1, 0)
    scatter_z(1, 2)
    scatter_ahead(1, 1)
    scatter_z(1, 3)
    scatter_ahead(1, 0)
    scatter_z(1, 1)
    scatter_z(1, 0)
    finish_aggregate(0)
    finish_aggregate(1)

    pre = jnp.dot(agg[...], weight[...], preferred_element_type=F32) + bias[...]
    gate = jax.nn.sigmoid(pre)
    pre_grad = (cotangent[...].astype(F32) * gate * (1.0 + pre * (1.0 - gate))).astype(BF)
    grads = (g0, g1)
    for h in range(2):
        agg_grad = lax.dot_general(
            weight[h * H : (h + 1) * H, :], pre_grad, (((1,), (1,)), ((), ())), preferred_element_type=F32
        ).astype(BF)
        for t in range(2):
            grads[h][2 * col + t] = agg_grad[:, t * T : (t + 1) * T]

    gz = {}
    gx = {}

    def origin(k, d):
        return pl.ds(2 * col_at((0, 4 - side, 2, side)[k], d), 2)

    def spread(h, k):
        came = grads[h].at[origin(k, 0)]
        gx[h, k, 0] = send(came, came, gx_send.at[h, k, 0], gx_recv.at[h, k, 0], ahead)
        gx[h, k, 1] = send(came, came, gx_send.at[h, k, 1], gx_recv.at[h, k, 1], behind)
        if (h, k) in GRADS_X_STRAIGHT:
            gx[h, k, 2] = send(came, came, gx_send.at[h, k, 2], gx_recv.at[h, k, 2], far)

    def pass_on(h, k):
        if (h, k) in GRADS_X_STRAIGHT:
            return
        gx[h, k, 0].wait_recv()
        came = grads[h].at[origin(k, 4 - side)]
        gx[h, k, 2] = send(came, came, gx_send.at[h, k, 2], gx_recv.at[h, k, 2], ahead)

    def spread_z(h, k):
        straight = h in GRADS_Z_STRAIGHT
        block = grads[h].at[origin(1 if k == 2 and not straight else 0, 0)]
        device = (ahead_z, far_z if straight else ahead_z, behind_z)[k - 1]
        gz[h, k] = send(block, block, gz_send.at[h, k - 1], gz_recv.at[h, k - 1], device)

    def came_z(h, k):
        gz[h, k].wait_recv()
        if k == 1 and h not in GRADS_Z_STRAIGHT:
            spread_z(h, 2)
        spread(h, k)

    spread_z(0, 1)
    spread_z(0, 3)
    if 0 in GRADS_Z_STRAIGHT:
        spread_z(0, 2)
    spread(0, 0)
    spread(1, 0)

    activations[...] = (pre * gate).astype(BF)
    part = lax.dot_general(agg[...], pre_grad, (((0,), (0,)), ((), ())), preferred_element_type=F32)
    bias_part = jnp.broadcast_to(jnp.sum(pre_grad.astype(F32), axis=0, keepdims=True), (8, F))
    for n in range(32):
        ws[n // 16, n // 4 % 4, n % 4, 0:8, :] = part[8 * n : 8 * n + 8, :]
        ws[n // 16, n // 4 % 4, n % 4, 8:16, :] = bias_part
    stage = {}
    wnext = [0]

    def wsend(name, src, dst, device):
        n = wnext[0]
        wnext[0] += 1
        stage.setdefault(name, []).append(send(src, dst, w_send.at[n], w_recv.at[n], device))

    def landed(name):
        for copy in stage[name]:
            copy.wait_recv()

    def along_y(d):
        return (row_at(d, 0, 0), col)

    def along_x(d):
        return (row, col_at(0, d))

    def w_core():
        wsend("core", ws.at[1 - core], wc, sibling)

    def w_y():
        landed("core")
        for a in range(4):
            ws2[a] = ws[core, a] + wc[a]
        for d in range(1, 4):
            wsend("y", ws2.at[lax.rem(y + d, 4)], wy.at[y], along_y(d))
        wy[y] = ws2[y]

    def w_x():
        landed("y")
        ws3[...] = ((wy[0] + wy[1]) + wy[2]) + wy[3]
        for d in range(1, 4):
            wsend("x", ws3.at[lax.rem(x + d, 4)], wx.at[x], along_x(d))
        wx[x] = ws3[x]

    def w_zl():
        landed("x")
        ws4[0] = ((wx[0] + wx[1]) + wx[2]) + wx[3]
        wsend("zl", ws4.at[0], wl, (row_at(0, 1, 0), col))

    def w_zh():
        landed("zl")
        ws4[1] = ws4[0] + wl[...]
        for d in range(1, 4):
            wsend("zh", ws4.at[1], wz.at[zh], (row, col_at(d, 0)))
        wz[zh] = ws4[1]

    def v_x():
        landed("zh")
        total = ((wz[0] + wz[1]) + wz[2]) + wz[3]
        bias_grad[...] = total[8:9, :]
        wout[core, y, x] = total[0:8, :]
        at = wout.at[core, y, x]
        for d in range(1, 4):
            wsend("vx", at, at, along_x(d))

    def v_y():
        landed("vx")
        at = wout.at[core, y]
        for d in range(1, 4):
            wsend("vy", at, at, along_y(d))

    def v_core():
        landed("vy")
        at = wout.at[core]
        wsend("vcore", at, at, sibling)

    def v_end():
        landed("vcore")
        weight_grad[...] = wout[...].reshape(F, F)

    def gathered(h):
        for k in range(4):
            for d in range(3):
                gx[h, k, d].wait_recv()

    cr = (cr0, cr1)
    rsend = (rs0, rs1)
    rrecv = (rr0, rr1)
    ccopies = {}
    rcopies = {}
    order_out = chips + [(0, 0)]

    def scatter_core(h):
        for n, (dy, dz) in enumerate(order_out):
            block = row_at(dy, dz, 1)
            take(order, prefix[h], sums[h], block, True)
            at = pl.ds(2 * block, 2)
            ccopies[h, n] = send(sums[h].at[at], cr[h].at[n], c_send.at[h, n], c_recv.at[h, n], sibling)

    def scatter_row(h, at=range(8)):
        for n in at:
            dy, dz = order_out[n]
            block = row_at(dy, dz, 0)
            take(order, prefix[h], sums[h], block, True)
            ccopies[h, n].wait_recv()
            total = sums[h][pl.ds(2 * block, 2)].astype(F32) + cr[h][n].astype(F32)
            if n < 7:
                rsend[h][n] = total.astype(BF)
                rcopies[h, n] = send(
                    rsend[h].at[n], rrecv[h].at[n], r_send.at[h, n], r_recv.at[h, n], (row_at(dy, dz, 0), col)
                )
            else:
                own[h][...] = total

    def finish_feats(h):
        total = own[h][...]
        for n in range(7):
            rcopies[h, n].wait_recv()
            total += rrecv[h][n].astype(F32)
        for t in range(2):
            feats_grad[t * T : (t + 1) * T, h * H : (h + 1) * H] = total[t].T.astype(BF)

    w_core()
    pass_on(0, 0)
    came_z(0, 1)
    came_z(0, 3)
    pass_on(1, 0)
    spread_z(1, 1)
    spread_z(1, 3)
    if 1 in GRADS_Z_STRAIGHT:
        spread_z(1, 2)
    pass_on(0, 1)
    came_z(0, 2)
    pass_on(0, 3)
    w_y()
    came_z(1, 1)
    pass_on(0, 2)
    came_z(1, 3)
    w_x()
    for copy in xcopies.values():
        copy.wait_send()
    gathered(0)

    def more_1():
        pass_on(1, 1)
        came_z(1, 2)

    def more_2():
        pass_on(1, 3)
        w_zl()

    tile_sums(order, tiles, g0, p0, True, (more_1, more_2))
    pass_on(1, 2)
    scatter_core(0)
    w_zh()
    gathered(1)

    def row_1():
        scatter_row(0, range(4))

    def row_2():
        scatter_row(0, range(4, 8))
        v_x()

    tile_sums(order, tiles, g1, p1, True, (row_1, row_2))
    scatter_core(1)
    v_y()
    scatter_row(1)
    v_core()
    finish_feats(0)
    finish_feats(1)
    v_end()
    for copy in sends:
        copy.wait_send()


def copy_out(*refs):
    for n in range(4):
        refs[n + 4][...] = refs[n][...]


def body(node_feats, weight, bias, cotangent, tiles, coords, counts):
    vmem = pl.BlockSpec(memory_space=pltpu.VMEM)
    hbm = pl.BlockSpec(memory_space=pltpu.HBM)
    half = (TR, T, H)
    dma = pltpu.SemaphoreType.DMA
    pair = lambda shape, dtype=BF: [pltpu.VMEM(shape, dtype)] * 2
    both = lambda shape: [dma(shape), dma(shape)]
    outs = (
        jax.ShapeDtypeStruct((2 * T, F), BF),
        jax.ShapeDtypeStruct((F, F), F32),
        jax.ShapeDtypeStruct((1, F), F32),
        jax.ShapeDtypeStruct((2 * T, F), BF),
    )
    results = pl.pallas_call(
        kernel,
        out_shape=outs,
        in_specs=[hbm] * 6 + [pl.BlockSpec(memory_space=pltpu.SMEM)],
        out_specs=(vmem, vmem, vmem, vmem),
        scratch_shapes=[
            pltpu.VMEM((2 * T, F), BF),
            pltpu.VMEM((F, F), BF),
            pltpu.VMEM((1, F), F32),
            pltpu.VMEM((2 * T, F), BF),
            pltpu.VMEM((2, SLOTS), jnp.int32),
            pltpu.VMEM((SLOTS, T, T), BF),
            pltpu.VMEM((8, 256), jnp.int32),
            pltpu.SMEM((8, 256), jnp.int32),
            *pair((SLOTS, T, H)),
            *pair(half),
            *pair(half),
            *pair((4, 2, T, H)),
            *pair((4, 2, T, H)),
            *pair((4, 2, T, H)),
            *pair((4, 2, T, H)),
            *pair((3, 2, T, H)),
            *pair((3, 2, T, H)),
            *pair((2, T, H), F32),
            pltpu.VMEM((2 * T, F), BF),
            *pair(half),
            *pair((8, 2, T, H)),
            *pair((7, 2, T, H)),
            *pair((7, 2, T, H)),
            pltpu.VMEM((2, 4, 4, 16, F), F32),
            pltpu.VMEM((4, 4, 16, F), F32),
            pltpu.VMEM((4, 4, 16, F), F32),
            pltpu.VMEM((4, 4, 16, F), F32),
            pltpu.VMEM((4, 16, F), F32),
            pltpu.VMEM((4, 16, F), F32),
            pltpu.VMEM((16, F), F32),
            pltpu.VMEM((2, 16, F), F32),
            pltpu.VMEM((4, 16, F), F32),
            pltpu.VMEM((2, 4, 4, 8, F), F32),
            dma((7,)),
            *both((2, 7)),
            *both((2, 8)),
            *both((2, 3, 4)),
            *both((2, 3)),
            *both((2, 3)),
            *both((2, 4, 3)),
            *both((2, 8)),
            *both((2, 7)),
            *both((18,)),
        ],
        compiler_params=pltpu.CompilerParams(
            collective_id=0, has_side_effects=True, vmem_limit_bytes=63 * 2**20
        ),
    )(node_feats, weight, bias.reshape(1, F), cotangent, tiles.reshape(SLOTS, T, T),
      coords.reshape(SLOTS, 2).T, counts)
    activations, weight_grad, bias_grad, feats_grad = pl.pallas_call(
        copy_out,
        out_shape=outs,
        in_specs=[vmem] * 4,
        out_specs=[vmem] * 4,
        compiler_params=pltpu.CompilerParams(vmem_limit_bytes=63 * 2**20),
    )(*results)
    return activations, weight_grad, bias_grad.reshape(F), feats_grad


def solution(mesh):
    return jax.shard_map(
        body,
        mesh=mesh,
        in_specs=(
            P(("col", "row"), None),
            P(),
            P(),
            P(("row", "col"), None),
            P("row", "col", None, None, None),
            P("row", "col", None, None),
            P("row", "col"),
        ),
        out_specs=(P(("row", "col"), None), P(), P(), P(("col", "row"), None)),
        check_vma=False,
    )
```
